256 devices in a mesh: wide: 64 (over x_lo, y, z), narrow: 4 (over x_hi, core).
Axes of the slice: x: 4 (x_hi: 2, x_lo: 2; x = x_hi * 2 + x_lo), y: 4, z: 8, core: 2. Of those that a mesh axis runs over, the one named last changes fastest.
Arguments:
- patches_in: bfloat16 [512, 64, 768], P('wide'), may hold values from -6 to 6
- w_up: bfloat16 [768, 3072], P(None, 'narrow'), may hold values from -0.21875 to 0.21875
- w_down: bfloat16 [3072, 768], P('narrow'), may hold values from -0.109375 to 0.109375
- captions: bfloat16 [512, 32, 768], P(('wide', 'narrow')), may hold values from -11 to 11
- labels: int32 [512], P(('wide', 'narrow')), may hold values from 0 to 511, each once
- lengths: int32 [512], P(('wide', 'narrow')), may hold values from 4 to 32
Outputs:
- grad_images: float32 [512, 64, 768], P(('wide', 'narrow'))
- grad_captions: float32 [512, 32, 768], P(('wide', 'narrow'))
The draws below stay inside these ranges and needn't reach their ends.
Inputs may be any that keep to these rules, and one draw needn't show every extreme that they name: `labels`: each image is named by exactly one caption.
All inputs are finite; a program needn't handle non-finite values.
Results may differ from the reference program's by a relative error of at most 0.019.
Values may be sent and summed in bfloat16 or wider, within the bound.
A program may use at most 192 MiB of HBM per device.

```python
import math
import jax
import jax.numpy as jnp
from jax import lax

D = 768
FF = 3072
PATCH = 64
TXT_TOK = 32
IMAGES = 512


def shared_patches(key):
    return jax.random.normal(jax.random.fold_in(key, 11), (IMAGES, PATCH, D), jnp.float32)


def draw_patches_in(key, part):
    base = shared_patches(key)
    field = jnp.clip(base, -6.0, 6.0)
    return field.astype(jnp.bfloat16)


def draw_captions(key, part):
    key = jax.random.fold_in(key, 2)
    text = jax.random.normal(key, (IMAGES, TXT_TOK, D), jnp.float32)
    text = jnp.clip(text, -6.0, 6.0)
    return text.astype(jnp.bfloat16)


def draw_lengths(key, part):
    key = jax.random.fold_in(key, 3)
    counts = jax.random.randint(key, (IMAGES,), 4, TXT_TOK + 1, dtype=jnp.int32)
    counts = counts.at[0].set(TXT_TOK)
    counts = counts.at[1].set(4)
    return counts


def steps_of(rng, dims, shards, low, largest):
    def one(axis_at, parts):
        heights = jax.random.uniform(jax.random.fold_in(jax.random.fold_in(rng, 6), axis_at), (parts,), jnp.float32, low / len(shards), largest / len(shards))
        return jnp.repeat(jnp.exp(heights), dims[axis_at] // parts).reshape((-1,) + (1,) * (len(dims) - axis_at - 1))

    level = one(*shards[0])
    for cut in shards[1:]:
        level = level * one(*cut)
    return level


def centred(own_key, shape, scale, limit, pieces=(), kind=jnp.bfloat16):
    factor_of = steps_of(own_key, shape, pieces, -0.22, 0.18) if pieces else 1.0
    values = jax.random.normal(own_key, shape, jnp.float32) * scale * factor_of
    return jnp.minimum(jnp.maximum(values, -limit), limit).astype(kind)


def setup_inputs(seed: int = 0) -> dict:
    key_list = jax.random.split(jax.random.key(seed), 7)
    return {
        "patches_in": draw_patches_in(jax.random.fold_in(key_list[6], 71), 0),
        "w_up": centred(key_list[1], (D, FF), D ** -0.5, 0.21875, ((1, 4),)),
        "w_down": centred(key_list[2], (FF, D), FF ** -0.5, 0.109375, ((0, 4),)),
        "captions": draw_captions(jax.random.fold_in(key_list[6], 71), 0),
        "labels": jax.random.permutation(key_list[4], IMAGES).astype(jnp.int32),
        "lengths": draw_lengths(jax.random.fold_in(key_list[6], 71), 0),
    }


SCORE_GAIN = 1.75
LOGIT_SCALE = 4.0
LOGIT_BIAS = -26.0
NORM_EPS = 1e-06
MASKED = -1e+30

def layer_norm(mixed):
    center = mixed - lax.optimization_barrier(jnp.mean(mixed, axis=-1, keepdims=True))
    spread = lax.optimization_barrier(jnp.mean(center * center, axis=-1, keepdims=True))
    return center * lax.rsqrt(spread + NORM_EPS)

def pair_terms(images, caption_part, label_part, length_part, image_base, num_patch):
    part_caps, num_tok, feature_dim = caption_part.shape
    num_rows = images.shape[0]
    num_images = num_rows // num_patch
    factor = SCORE_GAIN / math.sqrt(feature_dim)
    flat_text = caption_part.reshape(part_caps * num_tok, feature_dim)
    scores = jnp.dot(flat_text, images.T, preferred_element_type=jnp.float32) * factor
    scores = scores.reshape(part_caps, num_tok, num_images, num_patch)
    valid = (jnp.arange(num_tok, dtype=jnp.int32)[None, :] < length_part[:, None]).astype(jnp.float32)
    masked_scores = jnp.where(valid[:, :, None, None] > 0.5, scores, MASKED)
    patch_top = lax.optimization_barrier(jnp.max(masked_scores, axis=1, keepdims=True))
    patch_exp = jnp.exp(masked_scores - patch_top)
    patch_total = lax.optimization_barrier(jnp.sum(patch_exp, axis=1, keepdims=True))
    patch_pool = (patch_top + jnp.log(patch_total))[:, 0]
    patch_weight = patch_exp / patch_total
    token_top = lax.optimization_barrier(jnp.max(scores, axis=3, keepdims=True))
    token_exp = jnp.exp(scores - token_top)
    token_total = lax.optimization_barrier(jnp.sum(token_exp, axis=3, keepdims=True))
    token_pool = (token_top + jnp.log(token_total))[..., 0]
    token_weight = token_exp / token_total
    length_float = length_part.astype(jnp.float32)
    similarity = 0.5 * (lax.optimization_barrier(jnp.mean(patch_pool, axis=2)) + lax.optimization_barrier(jnp.sum(valid[:, :, None] * token_pool, axis=1)) / length_float[:, None])
    logit = LOGIT_SCALE * similarity + LOGIT_BIAS
    image_ids = image_base + jnp.arange(num_images, dtype=jnp.int32)
    sign = jnp.where(label_part[:, None] == image_ids[None, :], 1.0, -1.0).astype(jnp.float32)
    pair_grad = -sign * jax.nn.sigmoid(-sign * logit)
    token_share = valid / length_float[:, None]
    score_grad = 0.5 * LOGIT_SCALE * factor * pair_grad[:, None, :, None] * (patch_weight / num_patch + token_share[:, :, None, None] * token_weight)
    score_grad = score_grad.reshape(part_caps * num_tok, num_rows).astype(jnp.bfloat16)
    text_grad = jnp.dot(score_grad, images, preferred_element_type=jnp.float32).reshape(part_caps, num_tok, feature_dim)
    return (score_grad, text_grad)

def reference(patches_in, w_up, w_down, captions, labels, lengths):
    flat_in = patches_in.reshape(IMAGES * PATCH, D)
    hidden = jax.nn.gelu(jnp.dot(flat_in, w_up, preferred_element_type=jnp.float32)).astype(jnp.bfloat16)
    mixed = flat_in.astype(jnp.float32) + jnp.dot(hidden, w_down, preferred_element_type=jnp.float32)
    images = layer_norm(mixed).astype(jnp.bfloat16)
    group_caps = 8
    caption_groups = captions.reshape(IMAGES // group_caps, group_caps, TXT_TOK, D)
    label_groups = labels.reshape(IMAGES // group_caps, group_caps)
    length_groups = lengths.reshape(IMAGES // group_caps, group_caps)

    def visit(image_grad, inputs):
        caption_part, label_part, length_part = inputs
        score_grad, text_grad = pair_terms(images, caption_part, label_part, length_part, 0, PATCH)
        flat_text = caption_part.reshape(group_caps * TXT_TOK, D)
        image_grad = image_grad + jnp.dot(score_grad.T, flat_text, preferred_element_type=jnp.float32)
        return (image_grad, text_grad)
    start_grad = jnp.zeros((IMAGES * PATCH, D), jnp.float32)
    image_grad, text_grads = lax.scan(visit, start_grad, (caption_groups, label_groups, length_groups))
    return (image_grad.reshape(IMAGES, PATCH, D), text_grads.reshape(IMAGES, TXT_TOK, D))
```

```python
import functools
import math

import jax
import jax.numpy as jnp
from jax import lax
from jax.experimental import pallas as pl
from jax.experimental.pallas import tpu as pltpu
from jax.sharding import Mesh, PartitionSpec as P

D = 768
FACTOR = 1.75 / math.sqrt(768)
LN2 = math.log(2.0)
S2 = FACTOR / LN2


def lane_all(x, op):
    x = op(x, pltpu.roll(x, 64, 1))
    x = op(x, pltpu.roll(x, 32, 1))
    return x

def pair_block(s_ref, g_ref, r0, c0, gr0, len_row, lab_row, image_id):
    lane = lax.broadcasted_iota(jnp.int32, (8, 128), 1)
    tile = lax.broadcasted_iota(jnp.int32, (8, 128), 0)
    tok = tile * 4 + lane // 32
    valid = tok < len_row
    neg = jnp.where(valid, 0.0, -1e30).astype(jnp.float32)
    lenf = len_row.astype(jnp.float32)
    share = jnp.where(valid, 1.0 / lenf, 0.0)
    ss = []
    pm = None
    tms = []
    for k in range(8):
        s = s_ref[pl.ds(r0, 64), pl.ds(c0 + k * 128, 128)] * S2
        m = s + neg[k:k+1]
        pm = m if pm is None else jnp.maximum(pm, m)
        tms.append(jnp.max(s, axis=0, keepdims=True))
    pm = lane_all(pm, jnp.maximum)
    ps = None
    tss = []
    e1s, e2s = [], []
    for k in range(8):
        s = s_ref[pl.ds(r0, 64), pl.ds(c0 + k * 128, 128)] * S2
        e1 = jnp.exp2(s + neg[k:k+1] - pm)
        e2 = jnp.exp2(s - tms[k])
        ps = e1 if ps is None else ps + e1
        tss.append(jnp.sum(e2, axis=0, keepdims=True))
        e1s.append(e1); e2s.append(e2)
    ps = lane_all(ps, jnp.add)
    tm = jnp.concatenate(tms, axis=0)
    ts = jnp.concatenate(tss, axis=0)
    patch_pool = pm * LN2 + jnp.log(ps)
    token_pool = tm * LN2 + jnp.log(ts)
    a = jnp.sum(patch_pool, axis=0, keepdims=True) * (1.0 / 64)
    b = jnp.sum(token_pool * share, axis=0, keepdims=True)
    b = lane_all(b, jnp.add)
    logit = 4.0 * 0.5 * (a + b) - 26.0
    sign = jnp.where(lab_row == image_id, 1.0, -1.0).astype(jnp.float32)
    pg = -sign / (1.0 + jnp.exp(sign * logit))
    pg = pg * (2.0 * FACTOR)
    ca = (pg * (1.0 / 64)) / ps
    cb = pg * share / ts
    for k in range(8):
        g = e1s[k] * ca + e2s[k] * cb[k:k+1]
        g_ref[pl.ds(gr0, 64), pl.ds(c0 + k * 128, 128)] = g.astype(jnp.bfloat16)


def pair_kernel(img_ref, cap_ref, len_ref, lab_ref, base_ref, ig_ref, tg_ref, s_ref, g_ref):
    def chunk(q, _):
        r = pl.multiple_of(q * 256, 256)

        def sc(n, _):
            n0 = pl.multiple_of(n * 512, 512)
            s_ref[:, pl.ds(n0, 512)] = lax.dot_general(
                img_ref[pl.ds(r, 256), :], cap_ref[pl.ds(n0, 512), :], (((1,), (1,)), ((), ())),
                preferred_element_type=jnp.float32)
            return 0

        lax.fori_loop(0, 4, sc, 0)

        def el(b, _):
            i = b // 2
            r0 = pl.multiple_of(i * 64, 64)
            g0 = pl.multiple_of(r + r0, 64)
            grp = b % 2
            c0 = pl.multiple_of(grp * 1024, 1024)
            slot = q * 4 + i
            image_id = base_ref[0] + (slot // 2) * 8 + slot % 2
            pair_block(s_ref, g_ref, r0, c0, g0, len_ref[pl.ds(grp, 1), :], lab_ref[pl.ds(grp, 1), :], image_id)
            return 0

        lax.fori_loop(0, 8, el, 0)
        ig_ref[pl.ds(r, 256), :] = jnp.dot(
            g_ref[pl.ds(r, 256), :], cap_ref[...], preferred_element_type=jnp.float32)
        return 0

    lax.fori_loop(0, 4, chunk, 0)

    def tg(n, _):
        n0 = pl.multiple_of(n * 256, 256)
        tg_ref[pl.ds(n0, 256), :] = lax.dot_general(
            g_ref[:, pl.ds(n0, 256)], img_ref[...], (((0,), (0,)), ((), ())),
            preferred_element_type=jnp.float32)
        return 0

    lax.fori_loop(0, 8, tg, 0)


def pair_call(img, cap, ln, lab, base):
    return pl.pallas_call(
        pair_kernel,
        out_shape=(jax.ShapeDtypeStruct((1024, D), jnp.float32), jax.ShapeDtypeStruct((2048, D), jnp.float32)),
        in_specs=[pl.BlockSpec(memory_space=pltpu.VMEM)] * 4 + [pl.BlockSpec(memory_space=pltpu.SMEM)],
        out_specs=[pl.BlockSpec(memory_space=pltpu.VMEM)] * 2,
        scratch_shapes=[pltpu.VMEM((256, 2048), jnp.float32), pltpu.VMEM((1024, 2048), jnp.bfloat16)],
        compiler_params=pltpu.CompilerParams(vmem_limit_bytes=48 * 2**20),
    )(img, cap, ln, lab, base)


def layer_norm(mixed):
    center = mixed - jnp.mean(mixed, axis=-1, keepdims=True)
    spread = jnp.mean(center * center, axis=-1, keepdims=True)
    return center * lax.rsqrt(spread + 1e-6)


def shards(patches_in, w_up, w_down, captions, labels, lengths):
    capax = ("core", "xl", "y", "xh")
    n_i = lax.axis_index("xh") * 2 + lax.axis_index("core")
    cap_all = lax.all_gather(captions, capax, axis=0, tiled=True)
    meta = lax.all_gather(jnp.stack([labels, lengths], 1), capax, axis=0, tiled=True)
    cap_all = cap_all.reshape(2, 32, 32, D).transpose(0, 2, 1, 3).reshape(2048, D)
    lab = jnp.tile(meta[:, 0].reshape(2, 32), (1, 4))
    ln = jnp.tile(meta[:, 1].reshape(2, 32), (1, 4))
    flat_in = patches_in.reshape(512, D)
    hidden = jax.nn.gelu(jnp.dot(flat_in, w_up, preferred_element_type=jnp.float32)).astype(jnp.bfloat16)
    part = jnp.dot(hidden, w_down, preferred_element_type=jnp.float32)
    own = lax.psum_scatter(part, ("xh", "core"), scatter_dimension=0, tiled=True).astype(jnp.float32)
    own_in = lax.dynamic_slice_in_dim(flat_in, n_i * 128, 128, 0).astype(jnp.float32)
    image = layer_norm(own_in + own).astype(jnp.bfloat16)
    images = lax.all_gather(image, "z", axis=0, tiled=True)
    base = (((lax.axis_index("xl") * 4 + lax.axis_index("y")) * 8) * 8 + n_i * 2).astype(jnp.int32).reshape(1)
    ig, tg = pair_call(images, cap_all, ln, lab, base)
    ig = lax.psum_scatter(ig, "z", scatter_dimension=0, tiled=True).astype(jnp.float32)
    tg = tg.reshape(2, 32, 32, D).transpose(0, 2, 1, 3).reshape(2048, D)
    tg = lax.psum_scatter(tg, capax, scatter_dimension=0, tiled=True).astype(jnp.float32)
    return ig.reshape(2, 64, D), tg.reshape(2, 32, D)


def solution(mesh):
    grid = Mesh(mesh.devices.reshape(2, 4, 8, 2, 2), ("xl", "y", "z", "xh", "core"))
    wide = ("xl", "y", "z")
    narrow = ("xh", "core")
    both = wide + narrow
    return jax.shard_map(
        shards,
        mesh=grid,
        in_specs=(P(wide), P(None, narrow), P(narrow), P(both), P(both), P(both)),
        out_specs=(P(both), P(both)),
        check_vma=False,
    )
```
